256 devices in a mesh: gx: 4 (over y), gy: 8 (over x, z_hi), gz: 8 (over z_lo, core).
Axes of the slice: x: 4, y: 4, z: 8 (z_hi: 2, z_lo: 4; z = z_hi * 4 + z_lo), core: 2. Of those that a mesh axis runs over, the one named last changes fastest.
Arguments:
- inputs: bfloat16 [1024, 8192], P('gx', 'gy'), may hold values from -1.5 to 1.5
- out_grad: bfloat16 [1024, 8192], P('gx', 'gy'), may hold values from -1.5 to 1.5
- w_gate: bfloat16 [8192, 16384], P('gy', ('gx', 'gz')), may hold values from -0.25 to 0.25
- w_up: bfloat16 [8192, 16384], P('gy', ('gx', 'gz')), may hold values from -0.25 to 0.25
- w_down: bfloat16 [16384, 8192], P(('gx', 'gz'), 'gy'), may hold values from -0.046875 to 0.046875
Outputs:
- input_grad: bfloat16 [1024, 8192], P('gx', ('gy', 'gz'))
- gate_grad: bfloat16 [8192, 16384], P('gy', ('gx', 'gz'))
- up_grad: bfloat16 [8192, 16384], P('gy', ('gx', 'gz'))
- down_grad: bfloat16 [16384, 8192], P(('gx', 'gz'), 'gy')
The draws below stay inside these ranges and needn't reach their ends.
All inputs are finite; a program needn't handle non-finite values.
Results may differ from the reference program's by a relative error of at most 0.015.
Values may be sent and summed in bfloat16 or wider, within the bound.
No kernel may reach another device: no remote copies, remote signals or barrier semaphores. Data moves between devices by JAX's collectives and lax.ppermute only.
A program may use at most 128 MiB of HBM per device.

```python
import jax
import jax.numpy as jnp
from jax import lax

D = 8192
FF = 16384
TOK_DEV = 256
TOKENS = 1024
N_GX = 4


def block_scale(own_key, shape, split, least, top_value):
    gain, own = 1.0, jax.random.fold_in(own_key, 6)
    for dim, blocks in split:
        draws = jnp.exp(jax.random.uniform(jax.random.fold_in(own, dim), (blocks,), jnp.float32, least / len(split), top_value / len(split)))
        gain = gain * jnp.repeat(draws, shape[dim] // blocks).reshape([-1 if axis == dim else 1 for axis in range(len(shape))])
    return gain


def centred(own_key, dims, deviation, reach, shards=(), kind=jnp.bfloat16):
    drawn = deviation * jax.random.normal(own_key, dims, jnp.float32)
    if shards:
        drawn = drawn * block_scale(own_key, dims, shards, -0.22, 0.18)
    return jnp.clip(drawn, -reach, reach).astype(kind)


def setup_inputs(seed: int = 0) -> dict:
    arg_keys = jax.random.split(jax.random.key(seed), 6)
    inputs = centred(arg_keys[0], (TOKENS, D), 0.25, 1.5, ((0, 4), (1, 8)))
    out_grad = centred(arg_keys[1], (TOKENS, D), 0.25, 1.5, ((0, 4), (1, 8)))
    w_gate = centred(arg_keys[2], (D, FF), (D // 16) ** -0.5, 0.25, ((0, 8), (1, 32)))
    w_up = centred(arg_keys[3], (D, FF), (D // 16) ** -0.5, 0.25, ((0, 8), (1, 32)))
    w_down = centred(arg_keys[4], (FF, D), FF ** -0.5, 0.046875, ((0, 32), (1, 8)))
    return {"inputs": inputs, "out_grad": out_grad, "w_gate": w_gate, "w_up": w_up, "w_down": w_down}


def silu_parts(gate, up_val, grad_hidden):
    sigma = jax.nn.sigmoid(gate)
    active = gate * sigma
    hidden = (active * up_val).astype(jnp.bfloat16)
    grad_gate = (grad_hidden * up_val * sigma * (1.0 + gate * (1.0 - sigma))).astype(jnp.bfloat16)
    grad_up = (grad_hidden * active).astype(jnp.bfloat16)
    return hidden, grad_gate, grad_up


def block_sum(left, right):
    left_blocks = left.reshape(N_GX, TOK_DEV, left.shape[1])
    right_blocks = right.reshape(N_GX, TOK_DEV, right.shape[1])

    def one_block(carry, pair):
        left_part, right_part = pair
        product = jnp.dot(left_part.T, right_part, preferred_element_type=jnp.float32).astype(jnp.bfloat16)
        product = lax.optimization_barrier(product)
        return carry + product.astype(jnp.float32), None

    start = jnp.zeros((left.shape[1], right.shape[1]), jnp.float32)
    total, _ = lax.scan(one_block, start, (left_blocks, right_blocks))
    return total.astype(jnp.bfloat16)


def reference(inputs, out_grad, w_gate, w_up, w_down):
    gate = jnp.dot(inputs, w_gate, preferred_element_type=jnp.float32)
    up_val = jnp.dot(inputs, w_up, preferred_element_type=jnp.float32)
    grad_hidden = jnp.dot(out_grad, w_down.T, preferred_element_type=jnp.float32)
    hidden, grad_gate, grad_up = silu_parts(gate, up_val, grad_hidden)
    down_grad = block_sum(hidden, out_grad)
    gate_grad = jnp.dot(inputs.T, grad_gate, preferred_element_type=jnp.float32).astype(jnp.bfloat16)
    up_grad = jnp.dot(inputs.T, grad_up, preferred_element_type=jnp.float32).astype(jnp.bfloat16)
    input_grad = jnp.dot(grad_gate, w_gate.T, preferred_element_type=jnp.float32) + jnp.dot(grad_up, w_up.T, preferred_element_type=jnp.float32)
    return input_grad.astype(jnp.bfloat16), gate_grad, up_grad, down_grad
```

```python
import jax
import jax.numpy as jnp
from jax import lax
from jax.experimental import pallas as pl
from jax.experimental.pallas import tpu as pltpu
from jax.sharding import Mesh, PartitionSpec as P

BF = jnp.bfloat16
F32 = jnp.float32
ROWS = 64
SIDE = ((0, 1), (2, 3))
BACK = ((1, 2), (3, 0))
FAR = ((0, 1),)


def both(pairs):
    return [q for a, b in pairs for q in ((a, b), (b, a))]


def swap(a, axis, pairs):
    return lax.ppermute(a, axis, both(pairs))


def turn(a, shift):
    return lax.ppermute(a, "y", [(i, (i + shift) % 4) for i in range(4)])


def dot(a, b, ca, cb):
    return lax.dot_general(a, b, (((ca,), (cb,)), ((), ())), preferred_element_type=F32)


def call(body, outs, args, flops=0, scratch=(), scalars=0):
    vmem = pl.BlockSpec(memory_space=pltpu.VMEM)
    smem = pl.BlockSpec(memory_space=pltpu.SMEM)
    size = sum(a.size * a.dtype.itemsize for a in args) + sum(
        jnp.dtype(o[1]).itemsize * o[0][0] * o[0][1] for o in outs
    )
    return pl.pallas_call(
        body,
        out_shape=[jax.ShapeDtypeStruct(s, d) for s, d in outs],
        in_specs=[smem] * scalars + [vmem] * (len(args) - scalars),
        out_specs=[vmem] * len(outs),
        scratch_shapes=list(scratch),
        compiler_params=pltpu.CompilerParams(vmem_limit_bytes=40 * 1024 * 1024),
        cost_estimate=pl.CostEstimate(flops=flops, bytes_accessed=size, transcendentals=0),
    )(*args)


def order_rows(place, x, dy, first, second):
    for j in range(4):
        rows = pl.ds(pl.multiple_of(place[j] * ROWS, ROWS), ROWS)
        to = first if j < 2 else second
        at = (j % 2) * ROWS
        to[at : at + ROWS, :] = x[rows, :]
        to[2 * ROWS + at : 3 * ROWS + at, :] = dy[rows, :]


def split_rows(value, send, keep, cols, kind):
    r = ROWS
    if kind == 0:
        keep[:, cols] = value[: 2 * r]
        send[:, cols] = value[2 * r :].astype(BF)
    else:
        keep[:r, cols] = value[:r]
        keep[r:, cols] = value[2 * r : 3 * r]
        send[:r, cols] = value[r : 2 * r].astype(BF)
        send[r:, cols] = value[3 * r :].astype(BF)


def partials(kind):
    def body(first, second, wg, wu, wd, send, keep):
        n = wg.shape[1]
        h = 2 * ROWS
        x = jnp.concatenate([first[:h], second[:h]], axis=0)
        split_rows(dot(x, wg[...], 1, 0), send, keep, slice(0, n), kind)
        split_rows(dot(x, wu[...], 1, 0), send, keep, slice(n, 2 * n), kind)
        dy = jnp.concatenate([first[h:], second[h:]], axis=0)
        split_rows(dot(dy, wd[...], 1, 1), send, keep, slice(2 * n, 3 * n), kind)

    return body


def halve(got, kept, send, keep):
    r = ROWS
    keep[...] = kept[:r] + got[:r].astype(F32)
    send[...] = (kept[r:] + got[r:].astype(F32)).astype(BF)


def add_round(got, kept, keep, send):
    total = kept[...] + got[...].astype(F32)
    keep[...] = total
    send[...] = total.astype(BF)


def silu_grads(got, kept, out):
    n = out.shape[1] // 3
    total = [kept[:, i * n : (i + 1) * n] + got[:, i * n : (i + 1) * n].astype(F32) for i in range(3)]
    gate, up, grad = total
    sigma = 1.0 / (1.0 + jnp.exp(-gate))
    active = gate * sigma
    out[:, :n] = (grad * up * sigma * (1.0 + gate * (1.0 - sigma))).astype(BF)
    out[:, n : 2 * n] = (grad * active).astype(BF)
    out[:, 2 * n :] = (active * up).astype(BF)


def input_partial(place, b0, b1, b2, b3, wg, wu, mine, other, full, held):
    n = wg.shape[1]
    for j, b in enumerate((b0, b1, b2, b3)):
        full[j * ROWS : (j + 1) * ROWS, :] = b[...]
    total = dot(full[:, :n], wg[...], 1, 1) + dot(full[:, n : 2 * n], wu[...], 1, 1)
    for j in range(4):
        rows = pl.ds(pl.multiple_of(place[j] * ROWS, ROWS), ROWS)
        held[rows, :] = total[j * ROWS : (j + 1) * ROWS]
    core = place[4]
    for k in range(4):
        cols = slice(k * 128, (k + 1) * 128)
        mine[:, cols] = held[:, pl.ds(pl.multiple_of((2 * k + core) * 128, 128), 128)]
        other[:, cols] = held[:, pl.ds(pl.multiple_of((2 * k + 1 - core) * 128, 128), 128)].astype(BF)


def add_cast(mine, got, out):
    out[...] = (mine[...] + got[...].astype(F32)).astype(BF)


def sum_blocks(place, mine, got, r1, r2, r3, keep, s1, s2, s3, held):
    held[...] = (
        mine[...] + got[...].astype(F32) + r1[...].astype(F32) + r2[...].astype(F32) + r3[...].astype(F32)
    )
    for k, to in enumerate((keep, s1, s2, s3)):
        to[...] = held[:, pl.ds(pl.multiple_of(place[5 + k] * 128, 128), 128)].astype(to.dtype)


def sum_last(keep, r1, r2, r3, out):
    out[...] = (keep[...] + r1[...].astype(F32) + r2[...].astype(F32) + r3[...].astype(F32)).astype(BF)


def weight_grads(*refs):
    tokens, grads, outs = refs[:8], refs[8:12], refs[12:15]
    n = outs[0].shape[1]
    h = 2 * ROWS
    full = jnp.concatenate([g[...] for g in grads], axis=0)
    for i in range(4):
        cols = slice(i * 256, (i + 1) * 256)
        x = jnp.concatenate([t[:h, cols] for t in tokens], axis=0)
        both_grads = dot(x, full[:, : 2 * n], 0, 0)
        outs[0][cols, :] = both_grads[:, :n].astype(BF)
        outs[1][cols, :] = both_grads[:, n:].astype(BF)
    dy = jnp.concatenate([t[h:, :] for t in tokens], axis=0)
    for i in range(2):
        cols = slice(i * 256, (i + 1) * 256)
        outs[2][cols, :] = dot(full[:, 2 * n + i * 256 : 2 * n + (i + 1) * 256], dy, 0, 0).astype(BF)


def local(inputs, out_grad, w_gate, w_up, w_down):
    rows, width = inputs.shape
    n = w_gate.shape[1]
    x, core, zl = lax.axis_index("x"), lax.axis_index("core"), lax.axis_index("zl")
    side = jnp.where((x == 1) | (x == 2), 1, 0)
    back = jnp.where(x >= 2, 1, 0)
    me = 2 * (side ^ core) + back
    place = jnp.stack([me, me ^ 1, me ^ 2, me ^ 3, core, zl, zl ^ 1, zl ^ 2, zl ^ 3]).astype(jnp.int32)

    first, second = call(order_rows, [((rows, width), BF)] * 2, (place, inputs, out_grad), scalars=1)
    chunks = [(first, second)]
    for shift in (-1, 1, 2):
        near = turn(first, shift)
        chunks.append((near, swap(near, "core", FAR)))

    kinds = (0, 1, 0, 1)
    axes = (SIDE, BACK)
    wide = 3 * n
    gathered = []
    for (a, b), kind in zip(chunks, kinds):
        one, two = axes[kind], axes[1 - kind]
        send, keep = call(
            partials(kind),
            [((2 * ROWS, wide), BF), ((2 * ROWS, wide), F32)],
            (a, b, w_gate, w_up, w_down),
            flops=2 * rows * width * wide,
        )
        got = swap(send, "x", one)
        send, keep = call(halve, [((ROWS, wide), BF), ((ROWS, wide), F32)], (got, keep))
        got = swap(send, "x", two)
        keep, send = call(add_round, [((ROWS, wide), F32), ((ROWS, wide), BF)], (got, keep))
        got = swap(send, "zh", FAR)
        (own,) = call(silu_grads, [((ROWS, wide), BF)], (got, keep))
        by_one, by_two = swap(own, "x", one), swap(own, "x", two)
        last = swap(by_one, "x", two)
        blocks = (own, by_two, by_one, last) if kind == 0 else (own, by_one, by_two, last)
        gathered.append(blocks)

    fulls, sums = [], []
    for blocks in gathered:
        mine, other, full = call(
            input_partial,
            [((rows, width // 2), F32), ((rows, width // 2), BF), ((rows, wide), BF)],
            (place, *blocks, w_gate, w_up),
            flops=2 * rows * width * 2 * n,
            scratch=[pltpu.VMEM((rows, width), F32)],
            scalars=1,
        )
        fulls.append(full)
        sums.append((mine, swap(other, "core", FAR)))

    arrived = []
    for (mine, got), shift in zip(sums[1:], (1, -1, 2)):
        (part,) = call(add_cast, [((rows, width // 2), BF)], (mine, got))
        arrived.append(turn(part, shift))
    gate_grad, up_grad, down_grad = call(
        weight_grads,
        [((width, n), BF), ((width, n), BF), ((n, width), BF)],
        (*[t for c in chunks for t in c], *fulls),
        flops=2 * 4 * rows * width * wide,
    )
    keep, *sends = call(
        sum_blocks,
        [((rows, 128), F32)] + [((rows, 128), BF)] * 3,
        (place, *sums[0], *arrived),
        scratch=[pltpu.VMEM((rows, width // 2), F32)],
        scalars=1,
    )
    last = [
        lax.ppermute(s, "zl", [(i, i ^ k) for i in range(4)]) for k, s in zip((1, 2, 3), sends)
    ]
    (input_grad,) = call(sum_last, [((rows, 128), BF)], (keep, *last))
    return input_grad, gate_grad, up_grad, down_grad


def solution(mesh):
    axes = ("y", "x", "zh", "zl", "core")
    fine = Mesh(mesh.devices.reshape(4, 4, 2, 4, 2), axes)
    tokens = P("y", ("x", "zh"))
    cols = P(("x", "zh"), ("y", "zl", "core"))
    lines = P(("y", "zl", "core"), ("x", "zh"))
    return jax.shard_map(
        local,
        mesh=fine,
        in_specs=(tokens, tokens, cols, cols, lines),
        out_specs=(P("y", ("x", "zh", "zl", "core")), cols, cols, lines),
        check_vma=False,
    )
```

```python
import jax
import jax.numpy as jnp
from jax import lax
from jax.experimental import pallas as pl
from jax.experimental.pallas import tpu as pltpu
from jax.sharding import Mesh, PartitionSpec as P

BF = jnp.bfloat16
F32 = jnp.float32
ROWS = 64
SIDE = ((0, 1), (2, 3))
BACK = ((1, 2), (3, 0))
ACROSS = ((0, 2), (1, 3))
FAR = ((0, 1),)


def both(pairs):
    return [q for a, b in pairs for q in ((a, b), (b, a))]


def swap(a, axis, pairs):
    return lax.ppermute(a, axis, both(pairs))


def turn(a, shift):
    return lax.ppermute(a, "y", [(i, (i + shift) % 4) for i in range(4)])


def dot(a, b, ca, cb):
    return lax.dot_general(a, b, (((ca,), (cb,)), ((), ())), preferred_element_type=F32)


def call(body, outs, args, scratch=(), scalars=0, after=(), same=None):
    vmem = pl.BlockSpec(memory_space=pltpu.VMEM)
    smem = pl.BlockSpec(memory_space=pltpu.SMEM)
    some = pl.BlockSpec(memory_space=pl.ANY)
    count = len(args)

    def run(*refs):
        body(*refs[:count], *refs[count + len(after) :])

    return pl.pallas_call(
        run,
        out_shape=[jax.ShapeDtypeStruct(s, d) for s, d in outs],
        in_specs=([smem] * scalars + [vmem] * (count - scalars) if same is None else [some] * count)
        + [some] * len(after),
        out_specs=[vmem if same is None else some] * len(outs),
        input_output_aliases={} if same is None else {same: 0},
        scratch_shapes=list(scratch),
        compiler_params=pltpu.CompilerParams(vmem_limit_bytes=40 * 1024 * 1024),
        cost_estimate=pl.CostEstimate(flops=0, bytes_accessed=0, transcendentals=0),
    )(*args, *after)


class Line:
    def __init__(self):
        self.last = ()

    def __call__(self, body, outs, args, wait=(), **options):
        result = call(body, outs, args, after=(*self.last, *wait), **options)
        self.last = (result[0],)
        return result

    def hold(self, value, *others):
        def nothing(*refs):
            pass

        result = call(nothing, [(value.shape, value.dtype)], (value, *others), after=self.last, same=0)
        self.last = (result[0],)
        return result[0]


def order_rows(place, x, dy, first, second):
    for j in range(4):
        rows = pl.ds(pl.multiple_of(place[j] * ROWS, ROWS), ROWS)
        to = first if j < 2 else second
        at = (j % 2) * ROWS
        to[at : at + ROWS, :] = x[rows, :]
        to[2 * ROWS + at : 3 * ROWS + at, :] = dy[rows, :]


def products(x, dy, weights, emit):
    r = ROWS
    wg, wu, wd = weights
    n = wg.shape[1]
    for k, (lhs, w, dim) in enumerate(((x, wg, 0), (x, wu, 0), (dy, wd, 1))):
        value = dot(lhs, w[...], 1, dim)
        for i in range(value.shape[0] // (4 * r)):
            emit(i, slice(k * n, (k + 1) * n), value[i * 4 * r : (i + 1) * 4 * r])


def spread_rows(sends, keep, base):
    r = ROWS

    def emit(i, cols, part):
        keep[i * r : (i + 1) * r, cols] = part[:r]
        for to, j in zip(sends, (2, 1, 3)):
            to[base + i * r : base + (i + 1) * r, cols] = part[j * r : (j + 1) * r].astype(BF)

    return emit


def partials(count):
    def body(*refs):
        pieces, refs = refs[: 2 * count], refs[2 * count :]
        wg, wu, wd, *sends, keep = refs
        h = 2 * ROWS
        x = jnp.concatenate([p[:h] for p in pieces], axis=0)
        dy = jnp.concatenate([p[h:] for p in pieces], axis=0)
        products(x, dy, (wg, wu, wd), spread_rows(sends, keep, 0))

    return body


def sum_and_partials(g1, g2, g3, kept, near, xs, ds, own, wg, wu, wd, send, keep, s1, s2, s3, last):
    block_sum(g1, g2, g3, kept, send, keep)
    h = 2 * ROWS
    for to in (s1, s2, s3):
        to[:ROWS, :] = own[...]
    x = jnp.concatenate([near[:h], xs[...]], axis=0)
    dy = jnp.concatenate([near[h:], ds[...]], axis=0)
    products(x, dy, (wg, wu, wd), spread_rows((s1, s2, s3), last, ROWS))


def cut(whole, top, low, again):
    h = 2 * ROWS
    top[...] = whole[:h]
    low[...] = whole[h:]
    again[...] = whole[...]


def block_sum(*refs):
    *got, kept, send, keep = refs
    tall = keep.shape[0]
    total = kept[...]
    for g in got:
        total = total + g[g.shape[0] - tall :, :].astype(F32)
    keep[...] = total
    send[...] = total.astype(BF)


def silu_grads(got, kept, out):
    n = out.shape[1] // 3
    total = [kept[:, i * n : (i + 1) * n] + got[:, i * n : (i + 1) * n].astype(F32) for i in range(3)]
    gate, up, grad = total
    sigma = 1.0 / (1.0 + jnp.exp(-gate))
    active = gate * sigma
    out[:, :n] = (grad * up * sigma * (1.0 + gate * (1.0 - sigma))).astype(BF)
    out[:, n : 2 * n] = (grad * active).astype(BF)
    out[:, 2 * n :] = (active * up).astype(BF)


def input_partial(place, own, from_side, from_back, from_across, wg, wu, other, mine, full, held):
    count = own.shape[0] // ROWS
    n = wg.shape[1]
    tall = 4 * ROWS
    for i in range(count):
        rows = slice(i * ROWS, (i + 1) * ROWS)
        for j, b in enumerate((own, from_back, from_side, from_across)):
            full[i * tall + j * ROWS : i * tall + (j + 1) * ROWS, :] = b[rows, :]
    total = dot(full[:, :n], wg[...], 1, 1) + dot(full[:, n : 2 * n], wu[...], 1, 1)
    for i in range(count):
        for j in range(4):
            rows = pl.ds(pl.multiple_of(i * tall + place[j] * ROWS, ROWS), ROWS)
            held[rows, :] = total[i * tall + j * ROWS : i * tall + (j + 1) * ROWS]
    core = place[4]
    for k in range(4):
        cols = slice(k * 128, (k + 1) * 128)
        mine[:, cols] = held[:, pl.ds(pl.multiple_of((2 * k + core) * 128, 128), 128)]
        other[:, cols] = held[:, pl.ds(pl.multiple_of((2 * k + 1 - core) * 128, 128), 128)].astype(BF)


def add_cast(mine, got, *outs):
    rows = outs[0].shape[0]
    for i, out in enumerate(outs):
        part = slice(i * rows, (i + 1) * rows)
        out[...] = (mine[part, :] + got[part, :].astype(F32)).astype(BF)


def sum_some(mine, got, r1, r2, out):
    out[...] = mine[...] + got[...].astype(F32) + r1[...].astype(F32) + r2[...].astype(F32)


def sum_near(place, mine, *refs):
    *near, s1, s2, s3, keep, held = refs
    total = mine[...]
    for r in near:
        total = total + r[...].astype(F32)
    held[...] = total
    for k, to in enumerate((keep, s1, s2, s3)):
        to[...] = held[:, pl.ds(pl.multiple_of(place[5 + k] * 128, 128), 128)].astype(to.dtype)


def sum_last(keep, *refs):
    *parts, out = refs
    total = keep[...]
    for p in parts:
        total = total + p[...].astype(F32)
    out[...] = total.astype(BF)


def weight_grads(*refs):
    tokens, (xs, ds), grads, outs = refs[:7], refs[7:9], refs[9:12], refs[12:15]
    n = outs[0].shape[1]
    h = 2 * ROWS
    full = jnp.concatenate([g[...] for g in grads], axis=0)
    for i in range(4):
        cols = slice(i * 256, (i + 1) * 256)
        x = jnp.concatenate([t[:h, cols] for t in tokens] + [xs[:, cols]], axis=0)
        both_grads = dot(x, full[:, : 2 * n], 0, 0)
        outs[0][cols, :] = both_grads[:, :n].astype(BF)
        outs[1][cols, :] = both_grads[:, n:].astype(BF)
    dy = jnp.concatenate([t[h:, :] for t in tokens] + [ds[...]], axis=0)
    for i in range(2):
        cols = slice(i * 256, (i + 1) * 256)
        outs[2][cols, :] = dot(full[:, 2 * n + i * 256 : 2 * n + (i + 1) * 256], dy, 0, 0).astype(BF)


def local(inputs, out_grad, w_gate, w_up, w_down):
    rows, width = inputs.shape
    n = w_gate.shape[1]
    x, core, zl = lax.axis_index("x"), lax.axis_index("core"), lax.axis_index("zl")
    side = jnp.where((x == 1) | (x == 2), 1, 0)
    back = jnp.where(x >= 2, 1, 0)
    me = 2 * (side ^ core) + back
    place = jnp.stack([me, me ^ 1, me ^ 2, me ^ 3, core, zl, zl ^ 1, zl ^ 2, zl ^ 3]).astype(jnp.int32)

    line = Line()
    wide = 3 * n

    def spread(blocks):
        return [swap(b, "x", pairs) for b, pairs in zip(blocks, (SIDE, BACK, ACROSS))]

    def partial(chunks):
        tall = len(chunks) * ROWS
        *sends, keep = line(
            partials(len(chunks)),
            [((tall, wide), BF)] * 3 + [((tall, wide), F32)],
            (*[c for pair in chunks for c in pair], w_gate, w_up, w_down),
        )
        return spread(sends), keep

    def far_sum(got, kept):
        send, keep = line(block_sum, [(kept.shape, BF), (kept.shape, F32)], (*got, kept))
        return swap(send, "zh", FAR), keep

    def nonlinear(got, kept, wait=()):
        (own,) = line(silu_grads, [(kept.shape, BF)], (got, kept), wait=wait)
        return own

    def back_input(own, got):
        tall = 4 * own.shape[0]
        other, mine, full = line(
            input_partial,
            [((tall, width // 2), BF), ((tall, width // 2), F32), ((tall, wide), BF)],
            (place, own, *got, w_gate, w_up),
            scratch=[pltpu.VMEM((tall, width), F32)],
            scalars=1,
        )
        return mine, swap(other, "core", FAR), full

    first, second = line(order_rows, [((rows, width), BF)] * 2, (place, inputs, out_grad), scalars=1)
    up_y, down_y = turn(first, -1), turn(first, 1)
    got0, keep0 = partial([(first, second)])
    far0, keep0 = far_sum(got0, keep0)
    up_y, down_y = line.hold(up_y), line.hold(down_y)
    chunk1 = (up_y, swap(up_y, "core", FAR))
    chunk2 = (down_y, swap(down_y, "core", FAR))
    first = line.hold(first)
    far_y = turn(first, 2)
    got12, keep12 = partial([chunk1, chunk2])
    own0 = nonlinear(far0, keep0)
    half = ((rows // 2, width), BF)
    top, low, far_y = line(cut, [half, half, ((rows, width), BF)], (far_y,))
    top, low = swap(top, "core", FAR), swap(low, "core", FAR)
    send, keep12, *sends, keep3 = line(
        sum_and_partials,
        [((2 * ROWS, wide), BF), ((2 * ROWS, wide), F32)] + [((2 * ROWS, wide), BF)] * 3 + [((ROWS, wide), F32)],
        (*got12, keep12, far_y, top, low, own0, w_gate, w_up, w_down),
    )
    far12, mixed = swap(send, "zh", FAR), spread(sends)
    far3, keep3 = far_sum(mixed, keep3)
    own12 = nonlinear(far12, keep12)
    all12 = spread([own12] * 3)
    mine0, other0, full0 = back_input(own0, mixed)
    own3 = nonlinear(far3, keep3)
    all3 = spread([own3] * 3)
    mine12, other12, full12 = back_input(own12, all12)
    parts = line(add_cast, [((rows, width // 2), BF)] * 2, (mine12, other12))
    r1, r2 = turn(parts[0], 1), turn(parts[1], -1)
    (some,) = line(sum_some, [((rows, width // 2), F32)], (mine0, other0, r1, r2))
    mine3, other3, full3 = back_input(own3, all3)
    parts = line(add_cast, [((rows, width // 2), BF)], (mine3, other3))
    near = [turn(parts[0], 2)]
    gate_grad, up_grad, down_grad = line(
        weight_grads,
        [((width, n), BF), ((width, n), BF), ((n, width), BF)],
        (first, second, *chunk1, *chunk2, far_y, top, low, full0, full12, full3),
    )
    *sends, keep = line(
        sum_near,
        [((rows, 128), BF)] * 3 + [((rows, 128), F32)],
        (place, some, *near),
        scratch=[pltpu.VMEM((rows, width // 2), F32)],
        scalars=1,
    )
    last = [lax.ppermute(s, "zl", [(i, i ^ k) for i in range(4)]) for k, s in zip((1, 2, 3), sends)]
    (input_grad,) = line(sum_last, [((rows, 128), BF)], (keep, *last))
    return input_grad, gate_grad, up_grad, down_grad


def solution(mesh):
    axes = ("y", "x", "zh", "zl", "core")
    fine = Mesh(mesh.devices.reshape(4, 4, 2, 4, 2), axes)
    tokens = P("y", ("x", "zh"))
    cols = P(("x", "zh"), ("y", "zl", "core"))
    lines = P(("y", "zl", "core"), ("x", "zh"))
    return jax.shard_map(
        local,
        mesh=fine,
        in_specs=(tokens, tokens, cols, cols, lines),
        out_specs=(P("y", ("x", "zh", "zl", "core")), cols, cols, lines),
        check_vma=False,
    )
```

```python
import jax
import jax.numpy as jnp
from jax import lax
from jax.experimental import pallas as pl
from jax.experimental.pallas import tpu as pltpu
from jax.sharding import Mesh, PartitionSpec as P

BF = jnp.bfloat16
F32 = jnp.float32
ROWS = 64
SIDE = ((0, 1), (2, 3))
BACK = ((1, 2), (3, 0))
ACROSS = ((0, 2), (1, 3))
FAR = ((0, 1),)


def both(pairs):
    return [q for a, b in pairs for q in ((a, b), (b, a))]


def swap(a, axis, pairs):
    return lax.ppermute(a, axis, both(pairs))


def turn(a, shift):
    return lax.ppermute(a, "y", [(i, (i + shift) % 4) for i in range(4)])


def dot(a, b, ca, cb):
    return lax.dot_general(a, b, (((ca,), (cb,)), ((), ())), preferred_element_type=F32)


def call(body, outs, args, scratch=(), scalars=0, after=(), same=None):
    vmem = pl.BlockSpec(memory_space=pltpu.VMEM)
    smem = pl.BlockSpec(memory_space=pltpu.SMEM)
    some = pl.BlockSpec(memory_space=pl.ANY)
    count = len(args)

    def run(*refs):
        body(*refs[:count], *refs[count + len(after) :])

    return pl.pallas_call(
        run,
        out_shape=[jax.ShapeDtypeStruct(s, d) for s, d in outs],
        in_specs=([smem] * scalars + [vmem] * (count - scalars) if same is None else [some] * count)
        + [some] * len(after),
        out_specs=[vmem if same is None else some] * len(outs),
        input_output_aliases={} if same is None else {same: 0},
        scratch_shapes=list(scratch),
        compiler_params=pltpu.CompilerParams(vmem_limit_bytes=40 * 1024 * 1024),
        cost_estimate=pl.CostEstimate(flops=0, bytes_accessed=0, transcendentals=0),
    )(*args, *after)


class Line:
    def __init__(self):
        self.last = ()

    def __call__(self, body, outs, args, wait=(), **options):
        result = call(body, outs, args, after=(*self.last, *wait), **options)
        self.last = (result[0],)
        return result

    def hold(self, value, *others):
        def nothing(*refs):
            pass

        result = call(nothing, [(value.shape, value.dtype)], (value, *others), after=self.last, same=0)
        self.last = (result[0],)
        return result[0]


def order_rows(place, x, dy, first, second):
    for j in range(4):
        rows = pl.ds(pl.multiple_of(place[j] * ROWS, ROWS), ROWS)
        to = first if j < 2 else second
        at = (j % 2) * ROWS
        to[at : at + ROWS, :] = x[rows, :]
        to[2 * ROWS + at : 3 * ROWS + at, :] = dy[rows, :]


def products(x, dy, weights, emit):
    r = ROWS
    wg, wu, wd = weights
    n = wg.shape[1]
    for k, (lhs, w, dim) in enumerate(((x, wg, 0), (x, wu, 0), (dy, wd, 1))):
        value = dot(lhs, w[...], 1, dim)
        for i in range(value.shape[0] // (4 * r)):
            emit(i, slice(k * n, (k + 1) * n), value[i * 4 * r : (i + 1) * 4 * r])


def spread_rows(sends, keep, base):
    r = ROWS

    def emit(i, cols, part):
        keep[i * r : (i + 1) * r, cols] = part[:r]
        for to, j in zip(sends, (2, 1, 3)):
            to[base + i * r : base + (i + 1) * r, cols] = part[j * r : (j + 1) * r].astype(BF)

    return emit


def partials(count):
    def body(*refs):
        pieces, refs = refs[: 2 * count], refs[2 * count :]
        wg, wu, wd, *sends, keep = refs
        h = 2 * ROWS
        x = jnp.concatenate([p[:h] for p in pieces], axis=0)
        dy = jnp.concatenate([p[h:] for p in pieces], axis=0)
        products(x, dy, (wg, wu, wd), spread_rows(sends, keep, 0))

    return body


def sum_and_partials(g1, g2, g3, kept, near, xs, ds, own, wg, wu, wd, send, keep, s1, s2, s3, last):
    block_sum(g1, g2, g3, kept, send, keep)
    h = 2 * ROWS
    for to in (s1, s2, s3):
        to[:ROWS, :] = own[...]
    x = jnp.concatenate([near[:h], xs[...]], axis=0)
    dy = jnp.concatenate([near[h:], ds[...]], axis=0)
    products(x, dy, (wg, wu, wd), spread_rows((s1, s2, s3), last, ROWS))


def cut(whole, top, low, again):
    h = 2 * ROWS
    top[...] = whole[:h]
    low[...] = whole[h:]
    again[...] = whole[...]


def block_sum(*refs):
    *got, kept, send, keep = refs
    tall = keep.shape[0]
    total = kept[...]
    for g in got:
        total = total + g[g.shape[0] - tall :, :].astype(F32)
    keep[...] = total
    send[...] = total.astype(BF)


def silu_grads(got, kept, *outs):
    n = got.shape[1] // 3
    gate, up, grad = (
        kept[:, i * n : (i + 1) * n] + got[:, i * n : (i + 1) * n].astype(F32) for i in range(3)
    )
    sigma = 1.0 / (1.0 + jnp.exp(-gate))
    active = gate * sigma
    outs[0][:, :n] = (grad * up * sigma * (1.0 + gate * (1.0 - sigma))).astype(BF)
    outs[0][:, n : 2 * n] = (grad * active).astype(BF)
    hidden = (active * up).astype(BF)
    if len(outs) == 1:
        outs[0][:, 2 * n :] = hidden
    else:
        outs[1][...] = hidden


def input_partial(place, own, from_side, from_back, from_across, wg, wu, *refs):
    *others, mine, full, held = refs
    count = own.shape[0] // ROWS
    n = wg.shape[1]
    tall = 4 * ROWS
    for i in range(count):
        rows = slice(i * ROWS, (i + 1) * ROWS)
        for j, b in enumerate((own, from_back, from_side, from_across)):
            full[i * tall + j * ROWS : i * tall + (j + 1) * ROWS, :] = b[rows, :]
    total = dot(full[:, :n], wg[...], 1, 1) + dot(full[:, n : 2 * n], wu[...], 1, 1)
    for i in range(count):
        for j in range(4):
            rows = pl.ds(pl.multiple_of(i * tall + place[j] * ROWS, ROWS), ROWS)
            held[rows, :] = total[i * tall + j * ROWS : i * tall + (j + 1) * ROWS]
    core = place[4]
    for k in range(4):
        cols = slice(k * 128, (k + 1) * 128)
        mine[:, cols] = held[:, pl.ds(pl.multiple_of((2 * k + core) * 128, 128), 128)]
        theirs = pl.ds(pl.multiple_of((2 * k + 1 - core) * 128, 128), 128)
        part = held.shape[0] // len(others)
        for i, other in enumerate(others):
            other[:, cols] = held[i * part : (i + 1) * part, theirs].astype(BF)


def add_cast(mine, got, *outs):
    rows = outs[0].shape[0]
    for i, out in enumerate(outs):
        part = slice(i * rows, (i + 1) * rows)
        out[...] = (mine[part, :] + got[part, :].astype(F32)).astype(BF)


def sum_some(mine, got, r1, r2, mine3, top, low, part, out):
    h = top.shape[0]
    part[:h, :] = (mine3[:h] + top[...].astype(F32)).astype(BF)
    part[h:, :] = (mine3[h:] + low[...].astype(F32)).astype(BF)
    out[...] = mine[...] + got[...].astype(F32) + r1[...].astype(F32) + r2[...].astype(F32)


def sum_near(place, mine, r3, send, keep, held):
    held[...] = mine[...] + r3[...].astype(F32)
    for k in range(2):
        cols = slice(k * 128, (k + 1) * 128)
        keep[:, cols] = held[:, pl.ds(pl.multiple_of(place[5 + k] * 128, 128), 128)]
        send[:, cols] = held[:, pl.ds(pl.multiple_of(place[7 + k] * 128, 128), 128)].astype(BF)


def sum_half(kept, got, send, keep):
    total = kept[...] + got[...].astype(F32)
    keep[...] = total[:, :128]
    send[...] = total[:, 128:].astype(BF)


def sum_last(keep, *refs):
    *parts, out = refs
    total = keep[...]
    for p in parts:
        total = total + p[...].astype(F32)
    out[...] = total.astype(BF)


def weight_grads(*refs):
    tokens, xs, grads, mark, outs = refs[:7], refs[7], refs[8:11], refs[11], refs[12:14]
    mark[...] = jnp.zeros_like(mark)
    n = outs[0].shape[1]
    h = 2 * ROWS
    full = jnp.concatenate([g[:, : 2 * n] for g in grads], axis=0)
    for i in range(4):
        cols = slice(i * 256, (i + 1) * 256)
        x = jnp.concatenate([t[:h, cols] for t in tokens] + [xs[:, cols]], axis=0)
        both_grads = dot(x, full, 0, 0)
        outs[0][cols, :] = both_grads[:, :n].astype(BF)
        outs[1][cols, :] = both_grads[:, n:].astype(BF)


def join(a, b, out):
    out[: a.shape[0], :] = a[...]
    out[a.shape[0] :, :] = b[...]


def down_grads(*refs):
    tokens, (ds, first, own, side, back, across, mark, out) = refs[:7], refs[7:]
    mark[...] = jnp.zeros_like(mark)
    n = out.shape[0]
    h, r = 2 * ROWS, ROWS
    pieces = [first[:, 2 * n :]]
    for i in range(3):
        pieces += [b[i * r : (i + 1) * r, :] for b in (own, back, side, across)]
    hidden = jnp.concatenate(pieces, axis=0)
    dy = jnp.concatenate([t[h:, :] for t in tokens] + [ds[...]], axis=0)
    for i in range(2):
        cols = slice(i * 256, (i + 1) * 256)
        out[cols, :] = dot(hidden[:, cols], dy, 0, 0).astype(BF)


def local(inputs, out_grad, w_gate, w_up, w_down):
    rows, width = inputs.shape
    n = w_gate.shape[1]
    x, core, zl = lax.axis_index("x"), lax.axis_index("core"), lax.axis_index("zl")
    side = jnp.where((x == 1) | (x == 2), 1, 0)
    back = jnp.where(x >= 2, 1, 0)
    me = 2 * (side ^ core) + back
    place = jnp.stack([me, me ^ 1, me ^ 2, me ^ 3, core, zl, zl ^ 1, zl ^ 2, zl ^ 3]).astype(jnp.int32)

    line = Line()
    wide = 3 * n

    def spread(blocks):
        return [swap(b, "x", pairs) for b, pairs in zip(blocks, (SIDE, BACK, ACROSS))]

    def partial(chunks):
        tall = len(chunks) * ROWS
        *sends, keep = line(
            partials(len(chunks)),
            [((tall, wide), BF)] * 3 + [((tall, wide), F32)],
            (*[c for pair in chunks for c in pair], w_gate, w_up, w_down),
        )
        return spread(sends), keep

    def far_sum(got, kept):
        send, keep = line(block_sum, [(kept.shape, BF), (kept.shape, F32)], (*got, kept))
        return swap(send, "zh", FAR), keep

    def nonlinear(got, kept, split=True):
        tall = kept.shape[0]
        shapes = [(tall, 2 * n), (tall, n)] if split else [(tall, wide)]
        return line(silu_grads, [(s, BF) for s in shapes], (got, kept))

    def back_input(own, got, parts=1):
        tall = 4 * own.shape[0]
        *others, mine, full = line(
            input_partial,
            [((tall // parts, width // 2), BF)] * parts
            + [((tall, width // 2), F32), ((tall, own.shape[1]), BF)],
            (place, own, *got, w_gate, w_up),
            scratch=[pltpu.VMEM((tall, width), F32)],
            scalars=1,
        )
        return mine, *[swap(o, "core", FAR) for o in others], full

    first, second = line(
        order_rows, [((rows, width), BF)] * 2, (place, inputs, out_grad), scalars=1
    )
    up_y, down_y = turn(first, -1), turn(first, 1)
    got0, keep0 = partial([(first, second)])
    far0, keep0 = far_sum(got0, keep0)
    up_y, down_y = line.hold(up_y), line.hold(down_y)
    chunk1 = (up_y, swap(up_y, "core", FAR))
    chunk2 = (down_y, swap(down_y, "core", FAR))
    first = line.hold(first)
    far_y = turn(first, 2)
    got12, keep12 = partial([chunk1, chunk2])
    (own0,) = nonlinear(far0, keep0, split=False)
    half = ((rows // 2, width), BF)
    top, low, far_y = line(cut, [half, half, ((rows, width), BF)], (far_y,))
    top, low = swap(top, "core", FAR), swap(low, "core", FAR)
    send, keep12, *sends, keep3 = line(
        sum_and_partials,
        [((2 * ROWS, wide), BF), ((2 * ROWS, wide), F32)] + [((2 * ROWS, wide), BF)] * 3 + [((ROWS, wide), F32)],
        (*got12, keep12, far_y, top, low, own0, w_gate, w_up, w_down),
    )
    far12, mixed = swap(send, "zh", FAR), spread(sends)
    own12, hidden12 = nonlinear(far12, keep12)
    all12 = spread([own12] * 3)
    far3, keep3 = far_sum(mixed, keep3)
    mine0, other0, full0 = back_input(own0, mixed)
    own3, hidden3 = nonlinear(far3, keep3)
    all3 = spread([own3] * 3)
    mine12, other12, full12 = back_input(own12, all12)
    parts = line(add_cast, [((rows, width // 2), BF)] * 2, (mine12, other12))
    r1, r2 = turn(parts[0], 1), turn(parts[1], -1)
    mine3, top3, low3, full3 = back_input(own3, all3, parts=2)
    part3, some = line(
        sum_some,
        [((rows, width // 2), BF), ((rows, width // 2), F32)],
        (mine0, other0, r1, r2, mine3, top3, low3),
    )
    r3 = turn(part3, 2)
    (hidden,) = line(join, [((3 * ROWS, n), BF)], (hidden12, hidden3))
    hiddens = spread([hidden] * 3)
    tokens = (first, second, *chunk1, *chunk2, far_y)
    mark = ((8, 128), F32)
    _, gate_grad, up_grad = line(
        weight_grads, [mark] + [((width, n), BF)] * 2, (*tokens, top, full0, full12, full3)
    )
    send, keep = line(
        sum_near,
        [((rows, 256), BF), ((rows, 256), F32)],
        (place, some, r3),
        scratch=[pltpu.VMEM((rows, width // 2), F32)],
        scalars=1,
    )
    got = lax.ppermute(send, "zl", [(i, i ^ 2) for i in range(4)])
    _, down_grad = line(down_grads, [mark, ((n, width), BF)], (*tokens, low, full0, hidden, *hiddens))
    send, keep = line(sum_half, [((rows, 128), BF), ((rows, 128), F32)], (keep, got))
    got = lax.ppermute(send, "zl", [(i, i ^ 1) for i in range(4)])
    (input_grad,) = line(sum_last, [((rows, 128), BF)], (keep, got))
    return input_grad, gate_grad, up_grad, down_grad


def solution(mesh):
    axes = ("y", "x", "zh", "zl", "core")
    fine = Mesh(mesh.devices.reshape(4, 4, 2, 4, 2), axes)
    tokens = P("y", ("x", "zh"))
    cols = P(("x", "zh"), ("y", "zl", "core"))
    lines = P(("y", "zl", "core"), ("x", "zh"))
    return jax.shard_map(
        local,
        mesh=fine,
        in_specs=(tokens, tokens, cols, cols, lines),
        out_specs=(P("y", ("x", "zh", "zl", "core")), cols, cols, lines),
        check_vma=False,
    )
```

```python
import jax
import jax.numpy as jnp
from jax import lax
from jax.experimental import pallas as pl
from jax.experimental.pallas import tpu as pltpu
from jax.sharding import Mesh, PartitionSpec as P

BF = jnp.bfloat16
F32 = jnp.float32
ROWS = 64
SIDE = ((0, 1), (2, 3))
BACK = ((1, 2), (3, 0))
ACROSS = ((0, 2), (1, 3))
FAR = ((0, 1),)


def both(pairs):
    return [q for a, b in pairs for q in ((a, b), (b, a))]


def swap(a, axis, pairs):
    return lax.ppermute(a, axis, both(pairs))


def turn(a, shift):
    return lax.ppermute(a, "y", [(i, (i + shift) % 4) for i in range(4)])


def dot(a, b, ca, cb):
    return lax.dot_general(a, b, (((ca,), (cb,)), ((), ())), preferred_element_type=F32)


def call(body, outs, args, scratch=(), scalars=0, after=(), same=None):
    vmem = pl.BlockSpec(memory_space=pltpu.VMEM)
    smem = pl.BlockSpec(memory_space=pltpu.SMEM)
    some = pl.BlockSpec(memory_space=pl.ANY)
    count = len(args)

    def run(*refs):
        body(*refs[:count], *refs[count + len(after) :])

    return pl.pallas_call(
        run,
        out_shape=[jax.ShapeDtypeStruct(s, d) for s, d in outs],
        in_specs=([smem] * scalars + [vmem] * (count - scalars) if same is None else [some] * count)
        + [some] * len(after),
        out_specs=[vmem if same is None else some] * len(outs),
        input_output_aliases={} if same is None else {same: 0},
        scratch_shapes=list(scratch),
        compiler_params=pltpu.CompilerParams(vmem_limit_bytes=40 * 1024 * 1024),
        cost_estimate=pl.CostEstimate(flops=0, bytes_accessed=0, transcendentals=0),
    )(*args, *after)


class Line:
    def __init__(self):
        self.last = ()

    def __call__(self, body, outs, args, wait=(), **options):
        result = call(body, outs, args, after=(*self.last, *wait), **options)
        self.last = (result[0],)
        return result

    def hold(self, value, *others):
        def nothing(*refs):
            pass

        result = call(nothing, [(value.shape, value.dtype)], (value, *others), after=self.last, same=0)
        self.last = (result[0],)
        return result[0]


def order_rows(place, x, dy, first, second):
    for j in range(4):
        rows = pl.ds(pl.multiple_of(place[j] * ROWS, ROWS), ROWS)
        to = first if j < 2 else second
        at = (j % 2) * ROWS
        to[at : at + ROWS, :] = x[rows, :]
        to[2 * ROWS + at : 3 * ROWS + at, :] = dy[rows, :]


def products(x, dy, weights, emit):
    r = ROWS
    wg, wu, wd = weights
    n = wg.shape[1]
    for k, (lhs, w, dim) in enumerate(((x, wg, 0), (x, wu, 0), (dy, wd, 1))):
        value = dot(lhs, w[...], 1, dim)
        for i in range(value.shape[0] // (4 * r)):
            emit(i, slice(k * n, (k + 1) * n), value[i * 4 * r : (i + 1) * 4 * r])


def spread_rows(sends, keep, base):
    r = ROWS

    def emit(i, cols, part):
        keep[i * r : (i + 1) * r, cols] = part[:r]
        for to, j in zip(sends, (2, 1, 3)):
            to[base + i * r : base + (i + 1) * r, cols] = part[j * r : (j + 1) * r].astype(BF)

    return emit


def partials(count):
    def body(*refs):
        pieces, refs = refs[: 2 * count], refs[2 * count :]
        wg, wu, wd, *sends, keep = refs
        h = 2 * ROWS
        x = jnp.concatenate([p[:h] for p in pieces], axis=0)
        dy = jnp.concatenate([p[h:] for p in pieces], axis=0)
        products(x, dy, (wg, wu, wd), spread_rows(sends, keep, 0))

    return body


def sum_and_partials(g1, g2, g3, kept, near, xs, ds, own, wg, wu, wd, send, keep, s1, s2, s3, last):
    block_sum(g1, g2, g3, kept, send, keep)
    h = 2 * ROWS
    for to in (s1, s2, s3):
        to[:ROWS, :] = own[...]
    x = jnp.concatenate([near[:h], xs[...]], axis=0)
    dy = jnp.concatenate([near[h:], ds[...]], axis=0)
    products(x, dy, (wg, wu, wd), spread_rows((s1, s2, s3), last, ROWS))


def cut(whole, top, low, again):
    h = 2 * ROWS
    top[...] = whole[:h]
    low[...] = whole[h:]
    again[...] = whole[...]


def block_sum(*refs):
    *got, kept, send, keep = refs
    tall = keep.shape[0]
    total = kept[...]
    for g in got:
        total = total + g[g.shape[0] - tall :, :].astype(F32)
    keep[...] = total
    send[...] = total.astype(BF)


def silu_grads(got, kept, *outs):
    n = got.shape[1] // 3
    gate, up, grad = (
        kept[:, i * n : (i + 1) * n] + got[:, i * n : (i + 1) * n].astype(F32) for i in range(3)
    )
    sigma = 1.0 / (1.0 + jnp.exp(-gate))
    active = gate * sigma
    outs[0][:, :n] = (grad * up * sigma * (1.0 + gate * (1.0 - sigma))).astype(BF)
    outs[0][:, n : 2 * n] = (grad * active).astype(BF)
    hidden = (active * up).astype(BF)
    if len(outs) == 1:
        outs[0][:, 2 * n :] = hidden
    else:
        outs[1][...] = hidden


def input_partial(place, own, from_side, from_back, from_across, wg, wu, *refs):
    *others, mine, full, held = refs
    count = own.shape[0] // ROWS
    n = wg.shape[1]
    tall = 4 * ROWS
    for i in range(count):
        rows = slice(i * ROWS, (i + 1) * ROWS)
        for j, b in enumerate((own, from_back, from_side, from_across)):
            full[i * tall + j * ROWS : i * tall + (j + 1) * ROWS, :] = b[rows, :]
    total = dot(full[:, :n], wg[...], 1, 1) + dot(full[:, n : 2 * n], wu[...], 1, 1)
    for i in range(count):
        for j in range(4):
            rows = pl.ds(pl.multiple_of(i * tall + place[j] * ROWS, ROWS), ROWS)
            held[rows, :] = total[i * tall + j * ROWS : i * tall + (j + 1) * ROWS]
    core = place[4]
    for k in range(4):
        cols = slice(k * 128, (k + 1) * 128)
        mine[:, cols] = held[:, pl.ds(pl.multiple_of((2 * k + core) * 128, 128), 128)]
        theirs = pl.ds(pl.multiple_of((2 * k + 1 - core) * 128, 128), 128)
        part = held.shape[0] // len(others)
        for i, other in enumerate(others):
            other[:, cols] = held[i * part : (i + 1) * part, theirs].astype(BF)


def add_cast(mine, got, *outs):
    rows = outs[0].shape[0]
    for i, out in enumerate(outs):
        part = slice(i * rows, (i + 1) * rows)
        out[...] = (mine[part, :] + got[part, :].astype(F32)).astype(BF)


def sum_some(mine, got, r1, r2, mine3, top, low, part, out):
    h = top.shape[0]
    part[:h, :] = (mine3[:h] + top[...].astype(F32)).astype(BF)
    part[h:, :] = (mine3[h:] + low[...].astype(F32)).astype(BF)
    out[...] = mine[...] + got[...].astype(F32) + r1[...].astype(F32) + r2[...].astype(F32)


def sum_near(place, mine, r3, send, keep, held):
    held[...] = mine[...] + r3[...].astype(F32)
    for k in range(2):
        cols = slice(k * 128, (k + 1) * 128)
        keep[:, cols] = held[:, pl.ds(pl.multiple_of(place[5 + 2 * k] * 128, 128), 128)]
        send[:, cols] = held[:, pl.ds(pl.multiple_of(place[6 + 2 * k] * 128, 128), 128)].astype(BF)


def sum_half(kept, got, send, keep):
    total = kept[...] + got[...].astype(F32)
    keep[...] = total[:, :128]
    send[...] = total[:, 128:].astype(BF)


def sum_last(keep, *refs):
    *parts, out = refs
    total = keep[...]
    for p in parts:
        total = total + p[...].astype(F32)
    out[...] = total.astype(BF)


def weight_grads(*refs):
    tokens, xs, grads, mark, outs = refs[:7], refs[7], refs[8:11], refs[11], refs[12:14]
    mark[...] = jnp.zeros_like(mark)
    n = outs[0].shape[1]
    h = 2 * ROWS
    full = jnp.concatenate([g[:, : 2 * n] for g in grads], axis=0)
    for i in range(4):
        cols = slice(i * 256, (i + 1) * 256)
        x = jnp.concatenate([t[:h, cols] for t in tokens] + [xs[:, cols]], axis=0)
        both_grads = dot(x, full, 0, 0)
        outs[0][cols, :] = both_grads[:, :n].astype(BF)
        outs[1][cols, :] = both_grads[:, n:].astype(BF)


def join(a, b, out):
    out[: a.shape[0], :] = a[...]
    out[a.shape[0] :, :] = b[...]


def down_grads(*refs):
    tokens, (ds, first, own, side, back, across, mark, out) = refs[:7], refs[7:]
    mark[...] = jnp.zeros_like(mark)
    n = out.shape[0]
    h, r = 2 * ROWS, ROWS
    pieces = [first[:, 2 * n :]]
    for i in range(3):
        pieces += [b[i * r : (i + 1) * r, :] for b in (own, back, side, across)]
    hidden = jnp.concatenate(pieces, axis=0)
    dy = jnp.concatenate([t[h:, :] for t in tokens] + [ds[...]], axis=0)
    for i in range(2):
        cols = slice(i * 256, (i + 1) * 256)
        out[cols, :] = dot(hidden[:, cols], dy, 0, 0).astype(BF)


def local(inputs, out_grad, w_gate, w_up, w_down):
    rows, width = inputs.shape
    n = w_gate.shape[1]
    x, core, zl = lax.axis_index("x"), lax.axis_index("core"), lax.axis_index("zl")
    side = jnp.where((x == 1) | (x == 2), 1, 0)
    back = jnp.where(x >= 2, 1, 0)
    me = 2 * (side ^ core) + back
    place = jnp.stack([me, me ^ 1, me ^ 2, me ^ 3, core, zl, zl ^ 1, zl ^ 2, zl ^ 3]).astype(jnp.int32)

    line = Line()
    wide = 3 * n

    def spread(blocks):
        return [swap(b, "x", pairs) for b, pairs in zip(blocks, (SIDE, BACK, ACROSS))]

    def partial(chunks):
        tall = len(chunks) * ROWS
        *sends, keep = line(
            partials(len(chunks)),
            [((tall, wide), BF)] * 3 + [((tall, wide), F32)],
            (*[c for pair in chunks for c in pair], w_gate, w_up, w_down),
        )
        return spread(sends), keep

    def far_sum(got, kept):
        send, keep = line(block_sum, [(kept.shape, BF), (kept.shape, F32)], (*got, kept))
        return swap(send, "zh", FAR), keep

    def nonlinear(got, kept, split=True):
        tall = kept.shape[0]
        shapes = [(tall, 2 * n), (tall, n)] if split else [(tall, wide)]
        return line(silu_grads, [(s, BF) for s in shapes], (got, kept))

    def back_input(own, got, parts=1):
        tall = 4 * own.shape[0]
        *others, mine, full = line(
            input_partial,
            [((tall // parts, width // 2), BF)] * parts
            + [((tall, width // 2), F32), ((tall, own.shape[1]), BF)],
            (place, own, *got, w_gate, w_up),
            scratch=[pltpu.VMEM((tall, width), F32)],
            scalars=1,
        )
        return mine, *[swap(o, "core", FAR) for o in others], full

    first, second = line(
        order_rows, [((rows, width), BF)] * 2, (place, inputs, out_grad), scalars=1
    )
    up_y, down_y = turn(first, -1), turn(first, 1)
    got0, keep0 = partial([(first, second)])
    far0, keep0 = far_sum(got0, keep0)
    up_y, down_y = line.hold(up_y), line.hold(down_y)
    chunk1 = (up_y, swap(up_y, "core", FAR))
    chunk2 = (down_y, swap(down_y, "core", FAR))
    first = line.hold(first)
    far_y = turn(first, 2)
    got12, keep12 = partial([chunk1, chunk2])
    (own0,) = nonlinear(far0, keep0, split=False)
    half = ((rows // 2, width), BF)
    top, low, far_y = line(cut, [half, half, ((rows, width), BF)], (far_y,))
    top, low = swap(top, "core", FAR), swap(low, "core", FAR)
    send, keep12, *sends, keep3 = line(
        sum_and_partials,
        [((2 * ROWS, wide), BF), ((2 * ROWS, wide), F32)] + [((2 * ROWS, wide), BF)] * 3 + [((ROWS, wide), F32)],
        (*got12, keep12, far_y, top, low, own0, w_gate, w_up, w_down),
    )
    far12, mixed = swap(send, "zh", FAR), spread(sends)
    own12, hidden12 = nonlinear(far12, keep12)
    all12 = spread([own12] * 3)
    far3, keep3 = far_sum(mixed, keep3)
    mine0, other0, full0 = back_input(own0, mixed)
    own3, hidden3 = nonlinear(far3, keep3)
    all3 = spread([own3] * 3)
    mine12, other12, full12 = back_input(own12, all12)
    parts = line(add_cast, [((rows, width // 2), BF)] * 2, (mine12, other12))
    r1, r2 = turn(parts[0], 1), turn(parts[1], -1)
    mine3, top3, low3, full3 = back_input(own3, all3, parts=2)
    part3, some = line(
        sum_some,
        [((rows, width // 2), BF), ((rows, width // 2), F32)],
        (mine0, other0, r1, r2, mine3, top3, low3),
    )
    r3 = turn(part3, 2)
    (hidden,) = line(join, [((3 * ROWS, n), BF)], (hidden12, hidden3))
    hiddens = spread([hidden] * 3)
    tokens = (first, second, *chunk1, *chunk2, far_y)
    mark = ((8, 128), F32)
    _, gate_grad, up_grad = line(
        weight_grads, [mark] + [((width, n), BF)] * 2, (*tokens, top, full0, full12, full3)
    )
    send, keep = line(
        sum_near,
        [((rows, 256), BF), ((rows, 256), F32)],
        (place, some, r3),
        scratch=[pltpu.VMEM((rows, width // 2), F32)],
        scalars=1,
    )
    got = lax.ppermute(send, "zl", [(i, i ^ 1) for i in range(4)])
    _, down_grad = line(down_grads, [mark, ((n, width), BF)], (*tokens, low, full0, hidden, *hiddens))
    send, keep = line(sum_half, [((rows, 128), BF), ((rows, 128), F32)], (keep, got))
    got = lax.ppermute(send, "zl", [(i, i ^ 2) for i in range(4)])
    (input_grad,) = line(sum_last, [((rows, 128), BF)], (keep, got))
    return input_grad, gate_grad, up_grad, down_grad


def solution(mesh):
    axes = ("y", "x", "zh", "zl", "core")
    fine = Mesh(mesh.devices.reshape(4, 4, 2, 4, 2), axes)
    tokens = P("y", ("x", "zh"))
    cols = P(("x", "zh"), ("y", "zl", "core"))
    lines = P(("y", "zl", "core"), ("x", "zh"))
    return jax.shard_map(
        local,
        mesh=fine,
        in_specs=(tokens, tokens, cols, cols, lines),
        out_specs=(P("y", ("x", "zh", "zl", "core")), cols, cols, lines),
        check_vma=False,
    )
```
